32 devices in a mesh: grp: 8 (over y, x, core), mem: 4 (over z).
Axes of the slice: x: 2, y: 2, z: 4, core: 2. Of those that a mesh axis runs over, the one named last changes fastest.
Arguments:
- incident: bfloat16 [2, 256, 16384], P(None, None, ('grp', 'mem')), may hold values from -6 to 6
- near_blocks: bfloat16 [64, 3, 2, 256, 256], P(('grp', 'mem')), may hold values from -0.15625 to 0.15625
- near_mask: int32 [64, 3], P(('grp', 'mem')), may hold values 0 or 1
- far_source: int32 [8, 14], replicated, may hold values from 0 to 7
- far_rank: int32 [8, 14], P('grp'), may hold values from 32 to 128
- basis_in: bfloat16 [8, 4, 14, 2, 128, 512], P('grp', 'mem'), may hold values from -0.1875 to 0.1875
- section_one: bfloat16 [8, 4, 14, 2, 128, 256], P('grp', 'mem'), may hold values from -0.25 to 0.25
- section_two: bfloat16 [8, 4, 14, 2, 128, 256], P('grp', 'mem'), may hold values from -0.25 to 0.25
- basis_out: bfloat16 [8, 4, 14, 2, 2048, 128], P('grp', 'mem'), may hold values from -0.0625 to 0.0625
Outputs:
- product: bfloat16 [2, 256, 16384], P(None, None, ('grp', 'mem'))
The draws below stay inside these ranges and needn't reach their ends.
Inputs may be any that keep to these rules, and one draw needn't show every extreme that they name: far_source names the cluster whose coefficients feed each far-field block; clusters may repeat. far_rank gives the number of live rank components of each block. `near_mask`: 1 marks a present near-field block.
All inputs are finite; a program needn't handle non-finite values.
Results may differ from the reference program's by a relative error of at most 0.0053.
Values may be sent and summed in bfloat16 or wider, within the bound.
A program may use at most 128 MiB of HBM per device.

```python
import jax
import jax.numpy as jnp
import numpy as np
from jax import lax

ROWS_DEV = 512
NRHS = 256
RANK = 128
LEAF = 256
FAR = 14
GROUPS = 8
MEMBERS = 4
UNKNOWNS = 16384
LEAVES = 64


def plant(result, own_key, smallest, top_value):
    longest = result.shape.index(max(result.shape))
    spots = []
    for shift in (0, 1):
        where = [jax.random.randint(jax.random.fold_in(own_key, axis), (), 0, length) for axis, length in enumerate(result.shape)]
        where[longest] = (where[longest] + shift) % result.shape[longest]
        spots.append(tuple(where))
    return result.at[spots[0]].set(smallest).at[spots[1]].set(top_value)


def level_of(own_key, shape, split, smallest, largest):
    level = 1.0
    for axis_at, shards_of in split:
        heights = jax.random.uniform(jax.random.fold_in(jax.random.fold_in(own_key, 6), axis_at), (shards_of,), jnp.float32, smallest / len(split), largest / len(split))
        level = level * jnp.repeat(jnp.exp(heights), shape[axis_at] // shards_of).reshape((-1,) + (1,) * (len(shape) - 1 - axis_at))
    return level


def centred(stream_key, shape, width, limit, cuts=(), kind=jnp.bfloat16):
    drawn = jax.random.normal(stream_key, shape, jnp.float32) * width
    if len(cuts) > 0:
        drawn = level_of(stream_key, shape, cuts, -0.22, 0.18) * drawn
    return jnp.clip(drawn, min=-limit, max=limit).astype(kind)


def setup_inputs(seed: int = 0) -> dict:
    splits = jax.random.split(jax.random.key(seed), 10)
    return {
        "incident": centred(splits[0], (2, NRHS, UNKNOWNS), 1.0, 6.0, ((2, 32),)),
        "near_blocks": centred(splits[1], (LEAVES, 3, 2, LEAF, LEAF), (6 * LEAF) ** -0.5, 0.15625, ((0, 32),)),
        "near_mask": plant((jax.random.randint(splits[2], (LEAVES, 3), 0, 4) < 3).astype(jnp.int32), jax.random.fold_in(splits[2], 1), 0, 1),
        "far_source": plant(jax.random.randint(splits[3], (GROUPS, FAR), 0, GROUPS), jax.random.fold_in(splits[3], 1), 0, GROUPS - 1).astype(jnp.int32),
        "far_rank": plant(jax.random.randint(splits[4], (GROUPS, FAR), RANK // 4, RANK + 1), jax.random.fold_in(splits[4], 1), RANK // 4, RANK).astype(jnp.int32),
        "basis_in": centred(splits[5], (GROUPS, MEMBERS, FAR, 2, RANK, ROWS_DEV), (2 * ROWS_DEV) ** -0.5, 0.1875, ((0, 8), (1, 4))),
        "section_one": centred(splits[6], (GROUPS, MEMBERS, FAR, 2, RANK, 2 * RANK), (4 * RANK) ** -0.5, 0.25, ((0, 8), (1, 4))),
        "section_two": centred(splits[7], (GROUPS, MEMBERS, FAR, 2, RANK, 2 * RANK), (4 * RANK) ** -0.5, 0.25, ((0, 8), (1, 4))),
        "basis_out": centred(splits[8], (GROUPS, MEMBERS, FAR, 2, MEMBERS * ROWS_DEV, RANK), (4 * RANK * FAR) ** -0.5, 0.0625, ((0, 8), (1, 4))),
    }


def complex_apply(weight_real, weight_imag, vector_real, vector_imag, form):
    def mult(left, right):
        return jnp.einsum(form, left.astype(jnp.float32), right.astype(jnp.float32), precision=lax.Precision.HIGHEST)
    first = mult(weight_real, vector_real) - mult(weight_imag, vector_imag)
    second = mult(weight_real, vector_imag) + mult(weight_imag, vector_real)
    return first, second


def reference(incident, near_blocks, near_mask, far_source, far_rank, basis_in, section_one, section_two, basis_out):
    padded = jnp.pad(incident, ((0, 0), (0, 0), (LEAF, LEAF)))
    near_real = jnp.zeros((NRHS, LEAVES, LEAF), jnp.float32)
    near_imag = jnp.zeros((NRHS, LEAVES, LEAF), jnp.float32)
    for offset in range(3):
        window = padded[:, :, offset * LEAF: offset * LEAF + UNKNOWNS].reshape(2, NRHS, LEAVES, LEAF)
        first, second = complex_apply(near_blocks[:, offset, 0], near_blocks[:, offset, 1], window[0], window[1], "lab,nlb->nla")
        weight = near_mask[:, offset].astype(jnp.float32)[None, :, None]
        near_real = near_real + weight * first
        near_imag = near_imag + weight * second
    near = jnp.stack([near_real.reshape(NRHS, UNKNOWNS), near_imag.reshape(NRHS, UNKNOWNS)], 0)

    pieces = jnp.transpose(incident.reshape(2, NRHS, GROUPS, MEMBERS, ROWS_DEV), (2, 3, 0, 1, 4))
    members = np.arange(MEMBERS)

    def one_group(group):
        chosen = jnp.transpose(pieces[far_source[group]], (1, 0, 2, 3, 4))
        keep = (jnp.arange(RANK)[None, :] < far_rank[group][:, None]).astype(jnp.float32)
        keep = keep[None, :, None, :]
        first, second = complex_apply(basis_in[group][:, :, 0], basis_in[group][:, :, 1], chosen[:, :, 0], chosen[:, :, 1], "mfkr,mfnr->mfnk")
        level = jnp.stack([first * keep, second * keep], 2).astype(jnp.bfloat16)
        for bit, weights in ((0, section_one[group]), (1, section_two[group])):
            lower_index = members & ~(1 << bit)
            upper_index = members | (1 << bit)
            joined = jnp.concatenate([level[lower_index], level[upper_index]], -1)
            first, second = complex_apply(weights[:, :, 0], weights[:, :, 1], joined[:, :, 0], joined[:, :, 1], "mfkj,mfnj->mfnk")
            level = jnp.stack([first * keep, second * keep], 2).astype(jnp.bfloat16)
        outward = basis_out[group]
        first, second = complex_apply(outward[:, :, 0], outward[:, :, 1], level[:, :, 0], level[:, :, 1], "mfrk,mfnk->nr")
        return jnp.stack([first, second], 0)

    far = lax.map(one_group, jnp.arange(GROUPS, dtype=jnp.int32))
    far = jnp.transpose(far, (1, 2, 0, 3)).reshape(2, NRHS, UNKNOWNS)
    return (far + near).astype(jnp.bfloat16)
```

```python
import jax
import jax.numpy as jnp
from jax import lax
from jax.sharding import PartitionSpec as P

PARTS = 2


def partner_2(value, axis, stride):
    return lax.ppermute(value, axis, [(i, i ^ 1 << stride) for i in range(lax.axis_size(axis))])


def complex_apply(weight_real, weight_imag, vector_real, vector_imag, form):

    def mult(left, right):
        return jnp.einsum(form, left, right, preferred_element_type=jnp.float32)

    first = mult(weight_real, vector_real) - mult(weight_imag, vector_imag)
    second = mult(weight_real, vector_imag) + mult(weight_imag, vector_real)
    return (first, second)


def mix_section(level, partner, upper_bit, weights, keep):
    is_upper = upper_bit == 1
    lower_half = jnp.where(is_upper, partner, level)
    upper_half = jnp.where(is_upper, level, partner)
    joined = jnp.concatenate([lower_half, upper_half], -1)
    first, second = complex_apply(
        weights[:, 0], weights[:, 1], joined[:, 0], joined[:, 1], "fkj,fnj->fnk"
    )
    return jnp.stack([first * keep, second * keep], 1).astype(jnp.bfloat16)


def on_device(
    incident,
    near_blocks,
    near_mask,
    far_source,
    far_rank,
    basis_in,
    section_one,
    section_two,
    basis_out,
):
    nrhs_count = incident.shape[1]
    row_count = incident.shape[2]
    leaf_size = near_blocks.shape[3]
    leaf_count = near_blocks.shape[0]
    rank_size = basis_in.shape[4]
    group = lax.axis_index("grp")
    member = lax.axis_index("mem")
    bits = (member % 2, member // 2 % 2)
    count = lax.axis_size("grp") * lax.axis_size("mem")
    forward = [(i, i + 1) for i in range(count - 1)]
    backward = [(b, a) for a, b in forward]
    low = lax.ppermute(incident[:, :, row_count - leaf_size :], ("grp", "mem"), forward)
    high = lax.ppermute(incident[:, :, :leaf_size], ("grp", "mem"), backward)
    padded = jnp.concatenate([low, incident, high], axis=2)
    sources = lax.dynamic_slice_in_dim(far_source, group, 1, 0)[0]
    arrived = lax.all_gather(incident[None], "grp", axis=0, tiled=True)
    chosen = jnp.stack(
        [
            lax.dynamic_index_in_dim(arrived, sources[f], 0, keepdims=False)
            for f in range(far_source.shape[1])
        ]
    )
    near_real = jnp.zeros((nrhs_count, leaf_count, leaf_size), jnp.float32)
    near_imag = jnp.zeros((nrhs_count, leaf_count, leaf_size), jnp.float32)
    for offset in range(3):
        window = padded[:, :, offset * leaf_size : offset * leaf_size + row_count].reshape(
            2, nrhs_count, leaf_count, leaf_size
        )
        first, second = complex_apply(
            near_blocks[:, offset, 0],
            near_blocks[:, offset, 1],
            window[0],
            window[1],
            "lab,nlb->nla",
        )
        weight = near_mask[:, offset].astype(jnp.float32)[None, :, None]
        near_real = near_real + weight * first
        near_imag = near_imag + weight * second
    near = jnp.stack(
        [near_real.reshape(nrhs_count, row_count), near_imag.reshape(nrhs_count, row_count)], 0
    )
    keep = (jnp.arange(rank_size)[None, :] < far_rank[0][:, None]).astype(jnp.float32)[:, None, :]
    factor = basis_in[0, 0]
    outward = basis_out[0, 0]
    width = nrhs_count // PARTS
    pieces = []
    for part in range(PARTS):
        source = chosen[:, :, part * width : (part + 1) * width]
        first, second = complex_apply(
            factor[:, 0], factor[:, 1], source[:, 0], source[:, 1], "fkr,fnr->fnk"
        )
        level = jnp.stack([first * keep, second * keep], 1).astype(jnp.bfloat16)
        partner = partner_2(level, "mem", 0)
        level = mix_section(level, partner, bits[0], section_one[0, 0], keep)
        partner = partner_2(level, "mem", 1)
        level = mix_section(level, partner, bits[1], section_two[0, 0], keep)
        first, second = complex_apply(
            outward[:, 0], outward[:, 1], level[:, 0], level[:, 1], "frk,fnk->nr"
        )
        terms = jnp.stack([first, second], 0).reshape(2, width, 2, 2, row_count)
        sent = lax.dynamic_index_in_dim(terms, 1 - bits[0], 3, keepdims=False)
        held = lax.dynamic_index_in_dim(terms, bits[0], 3, keepdims=False)
        held = held + partner_2(sent.astype(jnp.bfloat16), "mem", 0).astype(jnp.float32)
        sent = lax.dynamic_index_in_dim(held, 1 - bits[1], 2, keepdims=False)
        held = lax.dynamic_index_in_dim(held, bits[1], 2, keepdims=False)
        held = held + partner_2(sent.astype(jnp.bfloat16), "mem", 1).astype(jnp.float32)
        pieces.append(held)
    far = jnp.concatenate(pieces, 1)
    return (far + near).astype(jnp.bfloat16)


def solution(mesh):
    placed = (
        P(None, None, ("grp", "mem")),
        P(("grp", "mem"), None, None, None, None),
        P(("grp", "mem"), None),
        P(),
        P("grp", None),
        P("grp", "mem", None, None, None, None),
        P("grp", "mem", None, None, None, None),
        P("grp", "mem", None, None, None, None),
        P("grp", "mem", None, None, None, None),
    )
    return jax.shard_map(
        on_device,
        mesh=mesh,
        in_specs=placed,
        out_specs=P(None, None, ("grp", "mem")),
        check_vma=False,
    )
```

```python
import functools

import jax
import jax.numpy as jnp
from jax import lax
from jax.experimental import pallas as pl
from jax.experimental.pallas import tpu as pltpu
from jax.sharding import PartitionSpec as P

MESH = pl.DeviceIdType.MESH
PARTS = 4
CUTS = 2


def dot_nt(left, right):
    return lax.dot_general(
        left, right, (((1,), (1,)), ((), ())), preferred_element_type=jnp.float32
    )


def kernel(
    groups,
    members,
    incident,
    near_blocks,
    near_mask,
    far_source,
    far_rank,
    basis_in,
    section_one,
    section_two,
    basis_out,
    out,
    arrived,
    halo,
    w_near,
    w_in,
    w_one,
    w_two,
    w_out,
    level0,
    level0p,
    level1,
    level1p,
    level2,
    near,
    held,
    send1,
    recv1,
    send2,
    recv2,
    load_sem,
    gather_send,
    gather_recv,
    halo_send,
    halo_recv,
    l0_send,
    l0_recv,
    l1_send,
    l1_recv,
    r1_send,
    r1_recv,
    r2_send,
    r2_recv,
):
    rhs, rows = incident.shape[1], incident.shape[2]
    leaves, leaf = near_blocks.shape[0], near_blocks.shape[3]
    far, rank = w_in.shape[0], w_in.shape[2]
    parts = level0.shape[0]
    width = rhs // parts
    cuts = l0_send.shape[0] // parts
    per = far // cuts
    units = parts * cuts
    tile = min(256, rows)
    tiles = rows // tile

    group = lax.axis_index("grp")
    member = lax.axis_index("mem")
    bit0 = lax.rem(member, 2)
    bit1 = lax.rem(member // 2, 2)
    across0 = {"mem": member + 1 - 2 * bit0}
    across1 = {"mem": member + 2 - 4 * bit1}
    count = groups * members
    flat = group * members + member
    after = lax.rem(flat + 1, count)
    before = lax.rem(flat + count - 1, count)
    after_id = {"grp": after // members, "mem": lax.rem(after, members)}
    before_id = {"grp": before // members, "mem": lax.rem(before, members)}
    bits = groups.bit_length() - 1
    group_bits = [lax.rem(group // (1 << b), 2) for b in range(bits)]

    def flipped(mask):
        value = group
        for b in range(bits):
            if mask >> b & 1:
                value = value + (1 - 2 * group_bits[b]) * (1 << b)
        return value

    own = pltpu.make_async_copy(incident, arrived.at[group], load_sem.at[0])
    own.start()
    loads = []
    for i, (source, target) in enumerate(
        (
            (basis_in.at[0, 0], w_in),
            (near_blocks, w_near),
            (section_one.at[0, 0], w_one),
            (section_two.at[0, 0], w_two),
            (basis_out.at[0, 0], w_out),
        )
    ):
        load = pltpu.make_async_copy(source, target, load_sem.at[i + 1])
        load.start()
        loads.append(load)
    load_in, load_near, load_one, load_two, load_out = loads

    barrier = pltpu.get_barrier_semaphore()
    greeted = [{"grp": flipped(1 << b)} for b in range(bits)]
    greeted += [across0, across1, after_id, before_id]
    for neighbour in greeted:
        pl.semaphore_signal(barrier, inc=1, device_id=neighbour, device_id_type=MESH)
    pl.semaphore_wait(barrier, len(greeted))

    started = []

    def send(source, target, send_sem, recv_sem, device):
        copy = pltpu.make_async_remote_copy(
            src_ref=source,
            dst_ref=target,
            send_sem=send_sem,
            recv_sem=recv_sem,
            device_id=device,
            device_id_type=MESH,
        )
        copy.start()
        started.append(copy)
        return copy

    halos = [
        send(
            incident.at[:, :, pl.ds(rows - leaf, leaf)],
            halo.at[0],
            halo_send.at[0],
            halo_recv.at[0],
            after_id,
        ),
        send(
            incident.at[:, :, pl.ds(0, leaf)],
            halo.at[1],
            halo_send.at[1],
            halo_recv.at[1],
            before_id,
        ),
    ]

    own.wait()
    outer = list(range(1, bits))
    orders = (outer, outer[::-1])
    number = [0, 0]

    def pass_on(half, mask, bit):
        slot = arrived.at[flipped(mask), half]
        j = number[half]
        number[half] += 1
        return send(
            slot, slot, gather_send.at[half, j], gather_recv.at[half, j], {"grp": flipped(1 << bit)}
        )

    masks = [[0], [0]]
    sideways = []
    pending = []
    for half in range(2):
        if outer:
            pending.append((half, [pass_on(half, 0, orders[half][0])]))
    for half in range(2):
        sideways.append(pass_on(half, 0, 0))
    for stage in range(len(outer)):
        later = []
        for half, copies in pending:
            for copy in copies:
                copy.wait_recv()
            fresh = [mask ^ 1 << orders[half][stage] for mask in masks[half]]
            masks[half] = masks[half] + fresh
            if stage + 1 < len(outer):
                later.append(
                    (half, [pass_on(half, mask, orders[half][stage + 1]) for mask in masks[half]])
                )
            for mask in fresh:
                sideways.append(pass_on(half, mask, 0))
        pending = later
    load_in.wait()
    for copy in sideways:
        copy.wait_recv()

    def combine(product):
        first = product[:width, :rank] - product[width:, rank:]
        second = product[width:, :rank] + product[:width, rank:]
        return first, second

    def kept(value, f):
        lanes = lax.broadcasted_iota(jnp.int32, value.shape, 1)
        return jnp.where(lanes < far_rank[0, f], value, 0.0)

    def stage_a(unit):
        part, cut = divmod(unit, cuts)

        def body(i, carry):
            f = cut * per + i
            x = arrived[far_source[group, f], :, part * width : (part + 1) * width, :]
            first, second = combine(
                dot_nt(x.reshape(2 * width, rows), w_in[f].reshape(2 * rank, rows))
            )
            level0[part, f, 0] = kept(first, f).astype(jnp.bfloat16)
            level0[part, f, 1] = kept(second, f).astype(jnp.bfloat16)
            return carry

        lax.fori_loop(0, per, body, 0)
        chunk = pl.ds(cut * per, per)
        return send(
            level0.at[part, chunk],
            level0p.at[part, chunk],
            l0_send.at[unit],
            l0_recv.at[unit],
            across0,
        )

    def mix(part, f, mine, theirs, weights, bit):
        x = jnp.concatenate(
            [mine[part, f].reshape(2 * width, rank), theirs[part, f].reshape(2 * width, rank)], 1
        )
        lower = pl.ds(pl.multiple_of(bit * rank, rank), rank)
        upper = pl.ds(pl.multiple_of((1 - bit) * rank, rank), rank)
        w = jnp.concatenate(
            [
                weights[f, :, :, lower].reshape(2 * rank, rank),
                weights[f, :, :, upper].reshape(2 * rank, rank),
            ],
            1,
        )
        first, second = combine(dot_nt(x, w))
        return kept(first, f).astype(jnp.bfloat16), kept(second, f).astype(jnp.bfloat16)

    def stage_b(unit):
        part, cut = divmod(unit, cuts)

        def body(i, carry):
            f = cut * per + i
            first, second = mix(part, f, level0, level0p, w_one, bit0)
            level1[part, f, 0] = first
            level1[part, f, 1] = second
            return carry

        lax.fori_loop(0, per, body, 0)
        chunk = pl.ds(cut * per, per)
        return send(
            level1.at[part, chunk],
            level1p.at[part, chunk],
            l1_send.at[unit],
            l1_recv.at[unit],
            across1,
        )

    def stage_d(unit):
        part, cut = divmod(unit, cuts)

        def body(i, carry):
            f = cut * per + i
            first, second = mix(part, f, level1, level1p, w_two, bit1)
            level2[f, :width, :rank] = first
            level2[f, :width, rank:] = -second
            level2[f, width:, :rank] = second
            level2[f, width:, rank:] = first
            return carry

        lax.fori_loop(0, per, body, 0)

    def outward(piece, t):
        at = pl.ds(pl.multiple_of(piece * rows + t * tile, tile), tile)
        w = jnp.concatenate(
            [w_out[f, c, at, :] for f in range(far) for c in range(2)], 1
        )
        x = jnp.concatenate([level2[f] for f in range(far)], 1)
        return dot_nt(x, w)

    def stage_e(part):
        def first_body(i, carry):
            high, t = i // tiles, lax.rem(i, tiles)
            value = outward(2 * high + 1 - bit0, t).astype(jnp.bfloat16)
            at = pl.ds(pl.multiple_of(t * tile, tile), tile)
            send1[part, high, 0, :, at] = value[:width]
            send1[part, high, 1, :, at] = value[width:]
            return carry

        lax.fori_loop(0, 2 * tiles, first_body, 0)
        copy = send(
            send1.at[part], recv1.at[part], r1_send.at[part], r1_recv.at[part], across0
        )

        def second_body(i, carry):
            high, t = i // tiles, lax.rem(i, tiles)
            value = outward(2 * high + bit0, t)
            at = pl.ds(pl.multiple_of(t * tile, tile), tile)
            held[part, high, 0, :, at] = value[:width]
            held[part, high, 1, :, at] = value[width:]
            return carry

        lax.fori_loop(0, 2 * tiles, second_body, 0)
        return copy

    def stage_f(part):
        away = held[part, 1 - bit1] + recv1[part, 1 - bit1].astype(jnp.float32)
        send2[part] = away.astype(jnp.bfloat16)
        copy = send(
            send2.at[part], recv2.at[part], r2_send.at[part], r2_recv.at[part], across1
        )
        near[part] += held[part, bit1] + recv1[part, bit1].astype(jnp.float32)
        return copy

    def stage_g(part):
        value = near[part] + recv2[part].astype(jnp.float32)
        out[:, part * width : (part + 1) * width, :] = value.astype(jnp.bfloat16)

    def near_field():
        has_before = jnp.where(flat > 0, 1, 0)
        has_after = jnp.where(flat < count - 1, 1, 0)

        def body(part, carry):
            at = pl.ds(pl.multiple_of(part * width, width), width)
            for i in range(leaves):
                real = jnp.zeros((width, leaf), jnp.float32)
                imag = jnp.zeros((width, leaf), jnp.float32)
                for offset in range(3):
                    j = i + offset - 1
                    weight = near_mask[i, offset]
                    if j < 0:
                        x = halo[0, :, at, :]
                        weight = weight * has_before
                    elif j >= leaves:
                        x = halo[1, :, at, :]
                        weight = weight * has_after
                    else:
                        x = arrived[group, :, at, j * leaf : (j + 1) * leaf]
                    product = dot_nt(
                        x.reshape(2 * width, leaf), w_near[i, offset].reshape(2 * leaf, leaf)
                    )
                    weight = weight.astype(jnp.float32)
                    real += weight * (product[:width, :leaf] - product[width:, leaf:])
                    imag += weight * (product[width:, :leaf] + product[:width, leaf:])
                near[part, 0, :, i * leaf : (i + 1) * leaf] = real
                near[part, 1, :, i * leaf : (i + 1) * leaf] = imag
            return carry

        lax.fori_loop(0, parts, body, 0)

    l0 = {}
    l1 = {}
    r1 = {}
    r2 = {}
    l0[0] = stage_a(0)
    if units > 1:
        l0[1] = stage_a(1)
    load_near.wait()
    for copy in halos:
        copy.wait_recv()
    near_field()
    load_one.wait()
    l0[0].wait_recv()
    l1[0] = stage_b(0)
    load_two.wait()
    load_out.wait()
    for unit in range(units):
        if unit + 2 < units:
            l0[unit + 2] = stage_a(unit + 2)
        if unit + 1 < units:
            l0[unit + 1].wait_recv()
            l1[unit + 1] = stage_b(unit + 1)
        l1[unit].wait_recv()
        stage_d(unit)
        part, cut = divmod(unit, cuts)
        if cut == cuts - 1:
            if part > 0:
                r1[part - 1].wait_recv()
                r2[part - 1] = stage_f(part - 1)
            r1[part] = stage_e(part)
    r1[parts - 1].wait_recv()
    r2[parts - 1] = stage_f(parts - 1)
    for part in range(parts):
        r2[part].wait_recv()
        stage_g(part)
    for copy in started:
        copy.wait_send()


def on_device(groups, members, *arrays):
    incident, near_blocks, near_mask, far_source, far_rank, basis_in, one, two, basis_out = arrays
    rhs, rows = incident.shape[1:]
    leaf = near_blocks.shape[3]
    far, _, rank = basis_in.shape[2:5]
    parts = PARTS
    cuts = CUTS if far % CUTS == 0 else 1
    width = rhs // parts
    units = parts * cuts
    bf16 = jnp.bfloat16
    dma = pltpu.SemaphoreType.DMA
    level = pltpu.VMEM((parts, far, 2, width, rank), bf16)
    sums = pltpu.VMEM((parts, 2, 2, width, rows), bf16)
    last = pltpu.VMEM((parts, 2, width, rows), bf16)
    somewhere = pl.BlockSpec(memory_space=pl.ANY)
    scalars = pl.BlockSpec(memory_space=pltpu.SMEM)
    return pl.pallas_call(
        functools.partial(kernel, groups, members),
        out_shape=jax.ShapeDtypeStruct(incident.shape, bf16),
        in_specs=[somewhere, somewhere, scalars, scalars, scalars] + [somewhere] * 4,
        out_specs=pl.BlockSpec(memory_space=pltpu.VMEM),
        scratch_shapes=[
            pltpu.VMEM((groups,) + incident.shape, bf16),
            pltpu.VMEM((2, 2, rhs, leaf), bf16),
            pltpu.VMEM(near_blocks.shape, bf16),
            pltpu.VMEM(basis_in.shape[2:], bf16),
            pltpu.VMEM(one.shape[2:], bf16),
            pltpu.VMEM(two.shape[2:], bf16),
            pltpu.VMEM(basis_out.shape[2:], bf16),
            level,
            level,
            level,
            level,
            pltpu.VMEM((far, 2 * width, 2 * rank), bf16),
            pltpu.VMEM((parts, 2, width, rows), jnp.float32),
            pltpu.VMEM((parts, 2, 2, width, rows), jnp.float32),
            sums,
            sums,
            last,
            last,
            dma((6,)),
            dma((2, groups)),
            dma((2, groups)),
            dma((2,)),
            dma((2,)),
            dma((units,)),
            dma((units,)),
            dma((units,)),
            dma((units,)),
            dma((parts,)),
            dma((parts,)),
            dma((parts,)),
            dma((parts,)),
        ],
        compiler_params=pltpu.CompilerParams(
            collective_id=0, has_side_effects=True, vmem_limit_bytes=62 * 1024 * 1024
        ),
    )(*arrays)


def solution(mesh):
    placed = (
        P(None, None, ("grp", "mem")),
        P(("grp", "mem"), None, None, None, None),
        P(("grp", "mem"), None),
        P(),
        P("grp", None),
        P("grp", "mem", None, None, None, None),
        P("grp", "mem", None, None, None, None),
        P("grp", "mem", None, None, None, None),
        P("grp", "mem", None, None, None, None),
    )
    return jax.shard_map(
        functools.partial(on_device, mesh.shape["grp"], mesh.shape["mem"]),
        mesh=mesh,
        in_specs=placed,
        out_specs=P(None, None, ("grp", "mem")),
        check_vma=False,
    )
```

```python
import functools

import jax
import jax.numpy as jnp
from jax import lax
from jax.experimental import pallas as pl
from jax.experimental.pallas import tpu as pltpu
from jax.sharding import PartitionSpec as P

MESH = pl.DeviceIdType.MESH
PARTS = 4
CUTS = 2


def dot_nt(left, right):
    return lax.dot_general(
        left, right, (((1,), (1,)), ((), ())), preferred_element_type=jnp.float32
    )


def kernel(
    groups,
    members,
    incident,
    near_blocks,
    near_mask,
    far_source,
    far_rank,
    basis_in,
    section_one,
    section_two,
    basis_out,
    out,
    halo,
    w_near,
    w_in,
    w_one,
    w_two,
    w_out,
    level0,
    level0p,
    level1,
    level1p,
    level2,
    near,
    held,
    send1,
    recv1,
    send2,
    recv2,
    load_sem,
    gather_send,
    gather_recv,
    halo_send,
    halo_recv,
    l0_send,
    l0_recv,
    l1_send,
    l1_recv,
    r1_send,
    r1_recv,
    r2_send,
    r2_recv,
    *arrived,
):
    rhs, rows = incident.shape[1], incident.shape[2]
    leaves, leaf = near_blocks.shape[0], near_blocks.shape[3]
    far, rank = w_in.shape[0], w_in.shape[2]
    parts = level0.shape[0]
    width = rhs // parts
    cuts = l0_send.shape[0] // parts
    per = far // cuts
    units = parts * cuts
    tile = min(256, rows)
    tiles = rows // tile

    group = lax.axis_index("grp")
    member = lax.axis_index("mem")
    bit0 = lax.rem(member, 2)
    bit1 = lax.rem(member // 2, 2)
    across0 = {"mem": member + 1 - 2 * bit0}
    across1 = {"mem": member + 2 - 4 * bit1}
    count = groups * members
    flat = group * members + member
    after = lax.rem(flat + 1, count)
    before = lax.rem(flat + count - 1, count)
    after_id = {"grp": after // members, "mem": lax.rem(after, members)}
    before_id = {"grp": before // members, "mem": lax.rem(before, members)}
    bits = groups.bit_length() - 1
    group_bits = [lax.rem(group // (1 << b), 2) for b in range(bits)]

    def flipped(mask):
        value = group
        for b in range(bits):
            if mask >> b & 1:
                value = value + (1 - 2 * group_bits[b]) * (1 << b)
        return value

    owns = [
        pltpu.make_async_copy(
            incident.at[:, pl.ds(part * width, width)], arrived[part].at[group], load_sem.at[5 + part]
        )
        for part in range(parts)
    ]
    for own in owns:
        own.start()
    loads = []
    for i, (source, target) in enumerate(
        (
            (basis_in.at[0, 0], w_in),
            (near_blocks, w_near),
            (section_one.at[0, 0], w_one),
            (section_two.at[0, 0], w_two),
            (basis_out.at[0, 0], w_out),
        )
    ):
        load = pltpu.make_async_copy(source, target, load_sem.at[i])
        load.start()
        loads.append(load)
    load_in, load_near, load_one, load_two, load_out = loads

    barrier = pltpu.get_barrier_semaphore()
    greeted = [{"grp": flipped(1 << b)} for b in range(bits)]
    greeted += [across0, across1, after_id, before_id]
    for neighbour in greeted:
        pl.semaphore_signal(barrier, inc=1, device_id=neighbour, device_id_type=MESH)
    pl.semaphore_wait(barrier, len(greeted))

    started = []

    def send(source, target, send_sem, recv_sem, device):
        copy = pltpu.make_async_remote_copy(
            src_ref=source,
            dst_ref=target,
            send_sem=send_sem,
            recv_sem=recv_sem,
            device_id=device,
            device_id_type=MESH,
        )
        copy.start()
        started.append(copy)
        return copy

    outer = list(range(1, bits))
    orders = (outer, outer[::-1])
    number = {}
    masks = {}
    sideways = {}
    pending = {}

    def pass_on(part, half, mask, bit):
        at = pl.ds(part * width, width)
        slot = arrived[part].at[flipped(mask), half]
        j = number.get((part, half), 0)
        number[part, half] = j + 1
        return send(
            incident.at[half, at] if mask == 0 else slot,
            slot,
            gather_send.at[part, half, j],
            gather_recv.at[part, half, j],
            {"grp": flipped(1 << bit)},
        )

    def gather(part, stage):
        if part >= parts or stage > len(outer):
            return
        for half in range(2):
            if stage == 0:
                masks[part, half] = [0]
                fresh = [0]
            else:
                for copy in pending[part, half]:
                    copy.wait_recv()
                fresh = [mask ^ 1 << orders[half][stage - 1] for mask in masks[part, half]]
                masks[part, half] = masks[part, half] + fresh
            if stage < len(outer):
                pending[part, half] = [
                    pass_on(part, half, mask, orders[half][stage]) for mask in masks[part, half]
                ]
            sideways.setdefault(part, []).extend(pass_on(part, half, mask, 0) for mask in fresh)

    def gathered(part):
        for stage in range(progress[part], len(outer) + 1):
            gather(part, stage)
        progress[part] = len(outer) + 1
        for copy in sideways.pop(part):
            copy.wait_recv()

    progress = [0] * parts

    def advance():
        for part in reversed(range(parts)):
            before_it = progress[part - 1] if part else len(outer) + 1
            if progress[part] <= len(outer) and progress[part] < before_it:
                gather(part, progress[part])
                progress[part] += 1

    advance()
    halos = [
        send(
            incident.at[:, :, pl.ds(rows - leaf, leaf)],
            halo.at[0],
            halo_send.at[0],
            halo_recv.at[0],
            after_id,
        ),
        send(
            incident.at[:, :, pl.ds(0, leaf)],
            halo.at[1],
            halo_send.at[1],
            halo_recv.at[1],
            before_id,
        ),
    ]

    for own in owns:
        own.wait()
    advance()
    load_in.wait()

    def combine(product):
        first = product[:width, :rank] - product[width:, rank:]
        second = product[width:, :rank] + product[:width, rank:]
        return first, second

    def kept(value, f):
        lanes = lax.broadcasted_iota(jnp.int32, value.shape, 1)
        return jnp.where(lanes < far_rank[0, f], value, 0.0)

    def stage_a(unit):
        part, cut = divmod(unit, cuts)

        def body(i, carry):
            f = cut * per + i
            x = arrived[part][far_source[group, f]]
            first, second = combine(
                dot_nt(x.reshape(2 * width, rows), w_in[f].reshape(2 * rank, rows))
            )
            level0[part, f, 0] = kept(first, f).astype(jnp.bfloat16)
            level0[part, f, 1] = kept(second, f).astype(jnp.bfloat16)
            return carry

        lax.fori_loop(0, per, body, 0)
        chunk = pl.ds(cut * per, per)
        return send(
            level0.at[part, chunk],
            level0p.at[part, chunk],
            l0_send.at[unit],
            l0_recv.at[unit],
            across0,
        )

    def mix(part, f, mine, theirs, weights, bit):
        x = jnp.concatenate(
            [mine[part, f].reshape(2 * width, rank), theirs[part, f].reshape(2 * width, rank)], 1
        )
        lower = pl.ds(pl.multiple_of(bit * rank, rank), rank)
        upper = pl.ds(pl.multiple_of((1 - bit) * rank, rank), rank)
        w = jnp.concatenate(
            [
                weights[f, :, :, lower].reshape(2 * rank, rank),
                weights[f, :, :, upper].reshape(2 * rank, rank),
            ],
            1,
        )
        first, second = combine(dot_nt(x, w))
        return kept(first, f).astype(jnp.bfloat16), kept(second, f).astype(jnp.bfloat16)

    def stage_b(unit):
        part, cut = divmod(unit, cuts)

        def body(i, carry):
            f = cut * per + i
            first, second = mix(part, f, level0, level0p, w_one, bit0)
            level1[part, f, 0] = first
            level1[part, f, 1] = second
            return carry

        lax.fori_loop(0, per, body, 0)
        chunk = pl.ds(cut * per, per)
        return send(
            level1.at[part, chunk],
            level1p.at[part, chunk],
            l1_send.at[unit],
            l1_recv.at[unit],
            across1,
        )

    def stage_d(unit):
        part, cut = divmod(unit, cuts)

        def body(i, carry):
            f = cut * per + i
            first, second = mix(part, f, level1, level1p, w_two, bit1)
            level2[f, :width, :rank] = first
            level2[f, :width, rank:] = -second
            level2[f, width:, :rank] = second
            level2[f, width:, rank:] = first
            return carry

        lax.fori_loop(0, per, body, 0)

    def outward(piece, t):
        at = pl.ds(pl.multiple_of(piece * rows + t * tile, tile), tile)
        w = jnp.concatenate(
            [w_out[f, c, at, :] for f in range(far) for c in range(2)], 1
        )
        x = jnp.concatenate([level2[f] for f in range(far)], 1)
        return dot_nt(x, w)

    def send_first(part, high, index):
        def body(t, carry):
            value = outward(2 * high + 1 - bit0, t).astype(jnp.bfloat16)
            at = pl.ds(pl.multiple_of(t * tile, tile), tile)
            send1[part, high, 0, :, at] = value[:width]
            send1[part, high, 1, :, at] = value[width:]
            return carry

        lax.fori_loop(0, tiles, body, 0)
        return send(
            send1.at[part, high],
            recv1.at[part, high],
            r1_send.at[2 * part + index],
            r1_recv.at[2 * part + index],
            across0,
        )

    def hold(part, high):
        def body(t, carry):
            value = outward(2 * high + bit0, t)
            at = pl.ds(pl.multiple_of(t * tile, tile), tile)
            held[part, high, 0, :, at] = value[:width]
            held[part, high, 1, :, at] = value[width:]
            return carry

        lax.fori_loop(0, tiles, body, 0)

    def send_second(part):
        away = held[part, 1 - bit1] + recv1[part, 1 - bit1].astype(jnp.float32)
        send2[part] = away.astype(jnp.bfloat16)
        return send(
            send2.at[part], recv2.at[part], r2_send.at[part], r2_recv.at[part], across1
        )

    def add_first(part):
        near[part] += held[part, bit1] + recv1[part, bit1].astype(jnp.float32)

    def stage_g(part):
        value = near[part] + recv2[part].astype(jnp.float32)
        out[:, part * width : (part + 1) * width, :] = value.astype(jnp.bfloat16)

    def near_field():
        has_before = jnp.where(flat > 0, 1, 0)
        has_after = jnp.where(flat < count - 1, 1, 0)

        for part in range(parts):
            at = pl.ds(part * width, width)
            for i in range(leaves):
                real = jnp.zeros((width, leaf), jnp.float32)
                imag = jnp.zeros((width, leaf), jnp.float32)
                for offset in range(3):
                    j = i + offset - 1
                    weight = near_mask[i, offset]
                    if j < 0:
                        x = halo[0, :, at, :]
                        weight = weight * has_before
                    elif j >= leaves:
                        x = halo[1, :, at, :]
                        weight = weight * has_after
                    else:
                        x = arrived[part][group, :, :, j * leaf : (j + 1) * leaf]
                    product = dot_nt(
                        x.reshape(2 * width, leaf), w_near[i, offset].reshape(2 * leaf, leaf)
                    )
                    weight = weight.astype(jnp.float32)
                    real += weight * (product[:width, :leaf] - product[width:, leaf:])
                    imag += weight * (product[width:, :leaf] + product[:width, leaf:])
                near[part, 0, :, i * leaf : (i + 1) * leaf] = real
                near[part, 1, :, i * leaf : (i + 1) * leaf] = imag

    l0 = {}
    l1 = {}
    r1 = {}
    r2 = {}

    def start_a(unit):
        if unit < units:
            if unit % cuts == 0:
                gathered(unit // cuts)
            l0[unit] = stage_a(unit)

    def second(part):
        r1[part][0].wait_recv()
        r2[part] = send_second(part)

    start_a(0)
    advance()
    start_a(1)
    advance()
    load_near.wait()
    load_one.wait()
    l0[0].wait_recv()
    l1[0] = stage_b(0)
    advance()
    for copy in halos:
        copy.wait_recv()
    near_field()
    load_two.wait()
    load_out.wait()
    for unit in range(units):
        advance()
        start_a(unit + 2)
        if unit + 1 < units:
            l0[unit + 1].wait_recv()
            l1[unit + 1] = stage_b(unit + 1)
        l1[unit].wait_recv()
        stage_d(unit)
        part, cut = divmod(unit, cuts)
        if cut == cuts - 1:
            r1[part] = (send_first(part, 1 - bit1, 0), send_first(part, bit1, 1))
            hold(part, 1 - bit1)
            if part > 0:
                second(part - 1)
                r1[part - 1][1].wait_recv()
                add_first(part - 1)
            if part == parts - 1:
                second(part)
            hold(part, bit1)
            if part > 1:
                r2[part - 2].wait_recv()
                stage_g(part - 2)
    r1[parts - 1][1].wait_recv()
    add_first(parts - 1)
    for part in range(max(parts - 2, 0), parts):
        r2[part].wait_recv()
        stage_g(part)
    for copy in started:
        copy.wait_send()


def on_device(groups, members, *arrays):
    incident, near_blocks, near_mask, far_source, far_rank, basis_in, one, two, basis_out = arrays
    rhs, rows = incident.shape[1:]
    leaf = near_blocks.shape[3]
    far, _, rank = basis_in.shape[2:5]
    parts = PARTS
    cuts = CUTS if far % CUTS == 0 else 1
    width = rhs // parts
    units = parts * cuts
    bf16 = jnp.bfloat16
    dma = pltpu.SemaphoreType.DMA
    level = pltpu.VMEM((parts, far, 2, width, rank), bf16)
    sums = pltpu.VMEM((parts, 2, 2, width, rows), bf16)
    last = pltpu.VMEM((parts, 2, width, rows), bf16)
    somewhere = pl.BlockSpec(memory_space=pl.ANY)
    scalars = pl.BlockSpec(memory_space=pltpu.SMEM)
    return pl.pallas_call(
        functools.partial(kernel, groups, members),
        out_shape=jax.ShapeDtypeStruct(incident.shape, bf16),
        in_specs=[somewhere, somewhere, scalars, scalars, scalars] + [somewhere] * 4,
        out_specs=pl.BlockSpec(memory_space=pltpu.VMEM),
        scratch_shapes=[
            pltpu.VMEM((2, 2, rhs, leaf), bf16),
            pltpu.VMEM(near_blocks.shape, bf16),
            pltpu.VMEM(basis_in.shape[2:], bf16),
            pltpu.VMEM(one.shape[2:], bf16),
            pltpu.VMEM(two.shape[2:], bf16),
            pltpu.VMEM(basis_out.shape[2:], bf16),
            level,
            level,
            level,
            level,
            pltpu.VMEM((far, 2 * width, 2 * rank), bf16),
            pltpu.VMEM((parts, 2, width, rows), jnp.float32),
            pltpu.VMEM((parts, 2, 2, width, rows), jnp.float32),
            sums,
            sums,
            last,
            last,
            dma((5 + parts,)),
            dma((parts, 2, 2 * groups)),
            dma((parts, 2, 2 * groups)),
            dma((2,)),
            dma((2,)),
            dma((units,)),
            dma((units,)),
            dma((units,)),
            dma((units,)),
            dma((2 * parts,)),
            dma((2 * parts,)),
            dma((parts,)),
            dma((parts,)),
        ]
        + [pltpu.VMEM((groups, 2, width, rows), bf16)] * parts,
        compiler_params=pltpu.CompilerParams(
            collective_id=0, has_side_effects=True, vmem_limit_bytes=62 * 1024 * 1024
        ),
    )(*arrays)


def solution(mesh):
    placed = (
        P(None, None, ("grp", "mem")),
        P(("grp", "mem"), None, None, None, None),
        P(("grp", "mem"), None),
        P(),
        P("grp", None),
        P("grp", "mem", None, None, None, None),
        P("grp", "mem", None, None, None, None),
        P("grp", "mem", None, None, None, None),
        P("grp", "mem", None, None, None, None),
    )
    return jax.shard_map(
        functools.partial(on_device, mesh.shape["grp"], mesh.shape["mem"]),
        mesh=mesh,
        in_specs=placed,
        out_specs=P(None, None, ("grp", "mem")),
        check_vma=False,
    )
```

```python
import functools

import jax
import jax.numpy as jnp
from jax import lax
from jax.experimental import pallas as pl
from jax.experimental.pallas import tpu as pltpu
from jax.sharding import PartitionSpec as P

MESH = pl.DeviceIdType.MESH
PARTS = 4
CUTS = 1


def dot_nt(left, right):
    return lax.dot_general(
        left, right, (((1,), (1,)), ((), ())), preferred_element_type=jnp.float32
    )


def kernel(
    groups,
    members,
    incident,
    near_blocks,
    near_mask,
    far_source,
    far_rank,
    basis_in,
    section_one,
    section_two,
    basis_out,
    out,
    halo,
    w_near,
    w_in,
    w_one,
    w_two,
    w_out,
    level0,
    level0p,
    level1,
    level1p,
    level2,
    near,
    held,
    send1,
    recv1,
    send2,
    recv2,
    load_sem,
    gather_send,
    gather_recv,
    halo_send,
    halo_recv,
    l0_send,
    l0_recv,
    l1_send,
    l1_recv,
    r1_send,
    r1_recv,
    r2_send,
    r2_recv,
    *arrived,
):
    rhs, rows = incident.shape[1], incident.shape[2]
    leaves, leaf = near_blocks.shape[0], near_blocks.shape[3]
    far, rank = w_in.shape[0], w_in.shape[2]
    parts = level0.shape[0]
    width = rhs // parts
    cuts = l0_send.shape[0] // parts
    per = far // cuts
    units = parts * cuts
    tile = min(256, rows)
    tiles = rows // tile

    group = lax.axis_index("grp")
    member = lax.axis_index("mem")
    bit0 = lax.rem(member, 2)
    bit1 = lax.rem(member // 2, 2)
    across0 = {"mem": member + 1 - 2 * bit0}
    across1 = {"mem": member + 2 - 4 * bit1}
    count = groups * members
    flat = group * members + member
    after = lax.rem(flat + 1, count)
    before = lax.rem(flat + count - 1, count)
    after_id = {"grp": after // members, "mem": lax.rem(after, members)}
    before_id = {"grp": before // members, "mem": lax.rem(before, members)}
    bits = groups.bit_length() - 1
    group_bits = [lax.rem(group // (1 << b), 2) for b in range(bits)]

    def flipped(mask):
        value = group
        for b in range(bits):
            if mask >> b & 1:
                value = value + (1 - 2 * group_bits[b]) * (1 << b)
        return value

    owns = [
        pltpu.make_async_copy(
            incident.at[:, pl.ds(part * width, width)], arrived[part].at[group], load_sem.at[5 + part]
        )
        for part in range(parts)
    ]
    for own in owns:
        own.start()
    loads = []
    for i, (source, target) in enumerate(
        (
            (basis_in.at[0, 0], w_in),
            (near_blocks, w_near),
            (section_one.at[0, 0], w_one),
            (section_two.at[0, 0], w_two),
            (basis_out.at[0, 0], w_out),
        )
    ):
        load = pltpu.make_async_copy(source, target, load_sem.at[i])
        load.start()
        loads.append(load)
    load_in, load_near, load_one, load_two, load_out = loads

    barrier = pltpu.get_barrier_semaphore()
    greeted = [{"grp": flipped(1 << b)} for b in range(bits)]
    greeted += [across0, across1, after_id, before_id]
    for neighbour in greeted:
        pl.semaphore_signal(barrier, inc=1, device_id=neighbour, device_id_type=MESH)
    pl.semaphore_wait(barrier, len(greeted))

    started = []

    def send(source, target, send_sem, recv_sem, device):
        copy = pltpu.make_async_remote_copy(
            src_ref=source,
            dst_ref=target,
            send_sem=send_sem,
            recv_sem=recv_sem,
            device_id=device,
            device_id_type=MESH,
        )
        copy.start()
        started.append(copy)
        return copy

    outer = list(range(1, bits))
    orders = (outer, outer[::-1])
    number = {}
    masks = {}
    sideways = {}
    pending = {}

    def pass_on(part, half, mask, bit):
        at = pl.ds(part * width, width)
        slot = arrived[part].at[flipped(mask), half]
        j = number.get((part, half), 0)
        number[part, half] = j + 1
        return send(
            incident.at[half, at] if mask == 0 else slot,
            slot,
            gather_send.at[part, half, j],
            gather_recv.at[part, half, j],
            {"grp": flipped(1 << bit)},
        )

    def gather(part, stage):
        if part >= parts or stage > len(outer):
            return
        for half in range(2):
            if stage == 0:
                masks[part, half] = [0]
                fresh = [0]
            else:
                for copy in pending[part, half]:
                    copy.wait_recv()
                fresh = [mask ^ 1 << orders[half][stage - 1] for mask in masks[part, half]]
                masks[part, half] = masks[part, half] + fresh
            if stage < len(outer):
                pending[part, half] = [
                    pass_on(part, half, mask, orders[half][stage]) for mask in masks[part, half]
                ]
            sideways.setdefault(part, []).extend(pass_on(part, half, mask, 0) for mask in fresh)

    def gathered(part):
        for stage in range(progress[part], len(outer) + 1):
            gather(part, stage)
        progress[part] = len(outer) + 1
        for copy in sideways.pop(part):
            copy.wait_recv()

    progress = [0] * parts

    def advance():
        for part in reversed(range(parts)):
            before_it = progress[part - 1] if part else len(outer) + 1
            if progress[part] <= len(outer) and progress[part] < before_it:
                gather(part, progress[part])
                progress[part] += 1

    advance()
    halos = [
        send(
            incident.at[:, :, pl.ds(rows - leaf, leaf)],
            halo.at[0],
            halo_send.at[0],
            halo_recv.at[0],
            after_id,
        ),
        send(
            incident.at[:, :, pl.ds(0, leaf)],
            halo.at[1],
            halo_send.at[1],
            halo_recv.at[1],
            before_id,
        ),
    ]

    for own in owns:
        own.wait()
    advance()
    load_in.wait()

    def combine(product):
        first = product[:width, :rank] - product[width:, rank:]
        second = product[width:, :rank] + product[:width, rank:]
        return first, second

    def kept(value, f):
        lanes = lax.broadcasted_iota(jnp.int32, value.shape, 1)
        return jnp.where(lanes < far_rank[0, f], value, 0.0)

    def stage_a(unit):
        part, cut = divmod(unit, cuts)

        def body(i, carry):
            f = cut * per + i
            x = arrived[part][far_source[group, f]]
            first, second = combine(
                dot_nt(x.reshape(2 * width, rows), w_in[f].reshape(2 * rank, rows))
            )
            level0[part, f, 0] = kept(first, f).astype(jnp.bfloat16)
            level0[part, f, 1] = kept(second, f).astype(jnp.bfloat16)
            return carry

        lax.fori_loop(0, per, body, 0)
        chunk = pl.ds(cut * per, per)
        return send(
            level0.at[part, chunk],
            level0p.at[part, chunk],
            l0_send.at[unit],
            l0_recv.at[unit],
            across0,
        )

    def mix(part, f, mine, theirs, weights, bit):
        x = jnp.concatenate(
            [mine[part, f].reshape(2 * width, rank), theirs[part, f].reshape(2 * width, rank)], 1
        )
        lower = pl.ds(pl.multiple_of(bit * rank, rank), rank)
        upper = pl.ds(pl.multiple_of((1 - bit) * rank, rank), rank)
        w = jnp.concatenate(
            [
                weights[f, :, :, lower].reshape(2 * rank, rank),
                weights[f, :, :, upper].reshape(2 * rank, rank),
            ],
            1,
        )
        first, second = combine(dot_nt(x, w))
        return kept(first, f).astype(jnp.bfloat16), kept(second, f).astype(jnp.bfloat16)

    def stage_b(unit):
        part, cut = divmod(unit, cuts)

        def body(i, carry):
            f = cut * per + i
            first, second = mix(part, f, level0, level0p, w_one, bit0)
            level1[part, f, 0] = first
            level1[part, f, 1] = second
            return carry

        lax.fori_loop(0, per, body, 0)
        chunk = pl.ds(cut * per, per)
        return send(
            level1.at[part, chunk],
            level1p.at[part, chunk],
            l1_send.at[unit],
            l1_recv.at[unit],
            across1,
        )

    def stage_d(unit):
        part, cut = divmod(unit, cuts)

        def body(i, carry):
            f = cut * per + i
            first, second = mix(part, f, level1, level1p, w_two, bit1)
            level2[f, :width, :rank] = first
            level2[f, :width, rank:] = -second
            level2[f, width:, :rank] = second
            level2[f, width:, rank:] = first
            return carry

        lax.fori_loop(0, per, body, 0)

    def outward(piece, t):
        at = pl.ds(pl.multiple_of(piece * rows + t * tile, tile), tile)
        w = jnp.concatenate(
            [w_out[f, c, at, :] for f in range(far) for c in range(2)], 1
        )
        x = jnp.concatenate([level2[f] for f in range(far)], 1)
        return dot_nt(x, w)

    def send_first(part, high, index):
        def body(t, carry):
            value = outward(2 * high + 1 - bit0, t).astype(jnp.bfloat16)
            at = pl.ds(pl.multiple_of(t * tile, tile), tile)
            send1[part, high, 0, :, at] = value[:width]
            send1[part, high, 1, :, at] = value[width:]
            return carry

        lax.fori_loop(0, tiles, body, 0)
        return send(
            send1.at[part, high],
            recv1.at[part, high],
            r1_send.at[2 * part + index],
            r1_recv.at[2 * part + index],
            across0,
        )

    def hold(part, high):
        def body(t, carry):
            value = outward(2 * high + bit0, t)
            at = pl.ds(pl.multiple_of(t * tile, tile), tile)
            held[part, high, 0, :, at] = value[:width]
            held[part, high, 1, :, at] = value[width:]
            return carry

        lax.fori_loop(0, tiles, body, 0)

    def send_second(part):
        away = held[part, 1 - bit1] + recv1[part, 1 - bit1].astype(jnp.float32)
        send2[part] = away.astype(jnp.bfloat16)
        return send(
            send2.at[part], recv2.at[part], r2_send.at[part], r2_recv.at[part], across1
        )

    def add_first(part):
        near[part] += held[part, bit1] + recv1[part, bit1].astype(jnp.float32)

    def stage_g(part):
        value = near[part] + recv2[part].astype(jnp.float32)
        out[:, part * width : (part + 1) * width, :] = value.astype(jnp.bfloat16)

    def near_field():
        has_before = jnp.where(flat > 0, 1, 0)
        has_after = jnp.where(flat < count - 1, 1, 0)

        for part in range(parts):
            at = pl.ds(part * width, width)
            for i in range(leaves):
                real = jnp.zeros((width, leaf), jnp.float32)
                imag = jnp.zeros((width, leaf), jnp.float32)
                for offset in range(3):
                    j = i + offset - 1
                    weight = near_mask[i, offset]
                    if j < 0:
                        x = halo[0, :, at, :]
                        weight = weight * has_before
                    elif j >= leaves:
                        x = halo[1, :, at, :]
                        weight = weight * has_after
                    else:
                        x = arrived[part][group, :, :, j * leaf : (j + 1) * leaf]
                    product = dot_nt(
                        x.reshape(2 * width, leaf), w_near[i, offset].reshape(2 * leaf, leaf)
                    )
                    weight = weight.astype(jnp.float32)
                    real += weight * (product[:width, :leaf] - product[width:, leaf:])
                    imag += weight * (product[width:, :leaf] + product[:width, leaf:])
                near[part, 0, :, i * leaf : (i + 1) * leaf] = real
                near[part, 1, :, i * leaf : (i + 1) * leaf] = imag

    l0 = {}
    l1 = {}
    r1 = {}
    r2 = {}

    def start_a(unit):
        if unit < units:
            if unit % cuts == 0:
                gathered(unit // cuts)
            l0[unit] = stage_a(unit)

    def second(part):
        r1[part][0].wait_recv()
        r2[part] = send_second(part)

    start_a(0)
    advance()
    start_a(1)
    advance()
    load_near.wait()
    load_one.wait()
    l0[0].wait_recv()
    l1[0] = stage_b(0)
    advance()
    for copy in halos:
        copy.wait_recv()
    near_field()
    load_two.wait()
    load_out.wait()
    for unit in range(units):
        advance()
        start_a(unit + 2)
        if unit + 1 < units:
            l0[unit + 1].wait_recv()
            l1[unit + 1] = stage_b(unit + 1)
        l1[unit].wait_recv()
        stage_d(unit)
        part, cut = divmod(unit, cuts)
        if cut == cuts - 1:
            r1[part] = (send_first(part, 1 - bit1, 0), send_first(part, bit1, 1))
            hold(part, 1 - bit1)
            if part > 0:
                second(part - 1)
                r1[part - 1][1].wait_recv()
                add_first(part - 1)
            if part == parts - 1:
                second(part)
            hold(part, bit1)
            if part > 1:
                r2[part - 2].wait_recv()
                stage_g(part - 2)
    r1[parts - 1][1].wait_recv()
    add_first(parts - 1)
    for part in range(max(parts - 2, 0), parts):
        r2[part].wait_recv()
        stage_g(part)
    for copy in started:
        copy.wait_send()


def on_device(groups, members, *arrays):
    incident, near_blocks, near_mask, far_source, far_rank, basis_in, one, two, basis_out = arrays
    rhs, rows = incident.shape[1:]
    leaf = near_blocks.shape[3]
    far, _, rank = basis_in.shape[2:5]
    parts = PARTS
    cuts = CUTS if far % CUTS == 0 else 1
    width = rhs // parts
    units = parts * cuts
    bf16 = jnp.bfloat16
    dma = pltpu.SemaphoreType.DMA
    level = pltpu.VMEM((parts, far, 2, width, rank), bf16)
    sums = pltpu.VMEM((parts, 2, 2, width, rows), bf16)
    last = pltpu.VMEM((parts, 2, width, rows), bf16)
    somewhere = pl.BlockSpec(memory_space=pl.ANY)
    scalars = pl.BlockSpec(memory_space=pltpu.SMEM)
    return pl.pallas_call(
        functools.partial(kernel, groups, members),
        out_shape=jax.ShapeDtypeStruct(incident.shape, bf16),
        in_specs=[somewhere, somewhere, scalars, scalars, scalars] + [somewhere] * 4,
        out_specs=pl.BlockSpec(memory_space=pltpu.VMEM),
        scratch_shapes=[
            pltpu.VMEM((2, 2, rhs, leaf), bf16),
            pltpu.VMEM(near_blocks.shape, bf16),
            pltpu.VMEM(basis_in.shape[2:], bf16),
            pltpu.VMEM(one.shape[2:], bf16),
            pltpu.VMEM(two.shape[2:], bf16),
            pltpu.VMEM(basis_out.shape[2:], bf16),
            level,
            level,
            level,
            level,
            pltpu.VMEM((far, 2 * width, 2 * rank), bf16),
            pltpu.VMEM((parts, 2, width, rows), jnp.float32),
            pltpu.VMEM((parts, 2, 2, width, rows), jnp.float32),
            sums,
            sums,
            last,
            last,
            dma((5 + parts,)),
            dma((parts, 2, 2 * groups)),
            dma((parts, 2, 2 * groups)),
            dma((2,)),
            dma((2,)),
            dma((units,)),
            dma((units,)),
            dma((units,)),
            dma((units,)),
            dma((2 * parts,)),
            dma((2 * parts,)),
            dma((parts,)),
            dma((parts,)),
        ]
        + [pltpu.VMEM((groups, 2, width, rows), bf16)] * parts,
        compiler_params=pltpu.CompilerParams(
            collective_id=0, has_side_effects=True, vmem_limit_bytes=62 * 1024 * 1024
        ),
    )(*arrays)


def solution(mesh):
    placed = (
        P(None, None, ("grp", "mem")),
        P(("grp", "mem"), None, None, None, None),
        P(("grp", "mem"), None),
        P(),
        P("grp", None),
        P("grp", "mem", None, None, None, None),
        P("grp", "mem", None, None, None, None),
        P("grp", "mem", None, None, None, None),
        P("grp", "mem", None, None, None, None),
    )
    return jax.shard_map(
        functools.partial(on_device, mesh.shape["grp"], mesh.shape["mem"]),
        mesh=mesh,
        in_specs=placed,
        out_specs=P(None, None, ("grp", "mem")),
        check_vma=False,
    )
```
